32 devices in a mesh: phase: 4 (over z), dp: 4 (over x, core), mp: 2 (over y).
Axes of the slice: x: 2, y: 2, z: 4, core: 2. Of those that a mesh axis runs over, the one named last changes fastest.
Arguments:
- enc_states: bfloat16 [4, 4, 256, 4096], P('phase', 'dp'), may hold values from -4 to 4
- queries: bfloat16 [4, 4, 128, 512], P('phase', 'dp', None, 'mp'), may hold values from -0.25 to 0.25
- query_segments: int32 [4, 4, 128], P('phase', 'dp'), may hold values from 0 to 7, as said below
- key_segments: int32 [4, 4, 256], P('phase', 'dp'), may hold values from 0 to 7, as said below
- kv_weight: bfloat16 [4, 4096, 2, 512], P('phase', None, None, 'mp'), may hold values from -0.09375 to 0.09375
- ctx_cotangent: bfloat16 [4, 4, 128, 512], P('phase', 'dp', None, 'mp'), may hold values from -16 to 16
Outputs:
- context: bfloat16 [4, 4, 128, 512], P('phase', 'dp', None, 'mp')
- state_grad: bfloat16 [4, 4, 256, 4096], P('phase', 'dp', 'mp')
- kv_weight_grad: bfloat16 [4, 4096, 2, 512], P('phase', 'dp', None, 'mp')
The draws below stay inside these ranges and needn't reach their ends.
Inputs may be any that keep to these rules, and one draw needn't show every extreme that they name: Along each row of query_segments and of key_segments the example numbers start at 0, never fall and rise by one at a time, every example holding one token or more; key_segments[s, r] and query_segments[s, r] hold the same number of examples; some row holds 8 examples. `key_segments`: see query_segments.
All inputs are finite; a program needn't handle non-finite values.
Results may differ from the reference program's by a relative error of at most 0.0095.
Values may be sent and summed in bfloat16 or wider, within the bound.
A program may use at most 64 MiB of HBM per device.

```python
import jax
import jax.numpy as jnp
from jax import lax

D = 4096
HEAD = 64
H_DEV = 4
HEADS = 8
INNER = 512
LEN_ENC = 256
LEN_DEC = 128
SEGS = 8
SECTIONS = 4
ROWS = 4


def permuted_cuts(row_key, length):
    return jax.random.permutation(row_key, length - 1)[:SEGS - 1]


def numbering(key, length, salt):
    counts = jax.random.randint(jax.random.fold_in(key, 101), (SECTIONS, ROWS), 2, SEGS + 1)
    counts = counts.at[0, 0].set(SEGS)
    row_keys = jax.random.split(jax.random.fold_in(key, salt), SECTIONS * ROWS)
    cuts = jax.vmap(partial_cuts(length))(row_keys) + 1
    live = jnp.arange(SEGS - 1)[None, :] < counts.reshape(-1, 1) - 1
    positions = jnp.arange(length)
    passed = (positions[None, :, None] >= cuts[:, None, :]) & live[:, None, :]
    return jnp.sum(passed.astype(jnp.int32), axis=-1).reshape(SECTIONS, ROWS, length).astype(jnp.int32)


def partial_cuts(length):

    def cutter(row_key):
        return permuted_cuts(row_key, length)
    return cutter


def draw_query_segments(key, part):
    return numbering(key, LEN_DEC, 7)


def draw_key_segments(key, part):
    return numbering(key, LEN_ENC, 13)


def block_scale(stream_key, dims, cuts, least, largest):
    level = 1.0
    for dim, shards_of in cuts:
        draws = jax.random.uniform(jax.random.fold_in(jax.random.fold_in(stream_key, 6), dim), (shards_of,), jnp.float32, least / len(cuts), largest / len(cuts))
        level = level * jnp.repeat(jnp.exp(draws), dims[dim] // shards_of).reshape((-1,) + (1,) * (len(dims) - 1 - dim))
    return level


def bell_draw(rng, dims, scale, reach, cuts=(), dtype=jnp.bfloat16):
    entries = scale * jax.random.normal(rng, dims, jnp.float32)
    if cuts:
        entries = entries * block_scale(rng, dims, cuts, -0.22, 0.18)
    return jnp.clip(entries, -reach, reach).astype(dtype)


def setup_inputs(seed: int = 0) -> dict:
    key_list = jax.random.split(jax.random.key(seed), 7)
    enc_states = bell_draw(key_list[0], (SECTIONS, ROWS, LEN_ENC, D), 1.0, 4.0, ((0, 4), (1, 4)))
    queries = jnp.clip(jax.random.uniform(key_list[1], (SECTIONS, ROWS, LEN_DEC, INNER), jnp.float32, -0.25, 0.25) * block_scale(key_list[1], (SECTIONS, ROWS, LEN_DEC, INNER), ((0, 4), (1, 4), (3, 2)), -0.4, 0.0), -0.25, 0.25).astype(jnp.bfloat16)
    query_segments = draw_query_segments(jax.random.fold_in(key_list[6], 71), 0)
    key_segments = draw_key_segments(jax.random.fold_in(key_list[6], 71), 0)
    kv_weight = bell_draw(key_list[4], (SECTIONS, D, 2, INNER), D ** -0.5, 0.09375, ((0, 4), (3, 2)))
    ctx_cotangent = bell_draw(key_list[5], (SECTIONS, ROWS, LEN_DEC, INNER), 4.0, 16.0, ((0, 4), (1, 4), (3, 2)))
    return {"enc_states": enc_states, "queries": queries, "query_segments": query_segments, "key_segments": key_segments, "kv_weight": kv_weight, "ctx_cotangent": ctx_cotangent}


def section(inputs):
    states, queries, query_segments, key_segments, kv_weight, ctx_cotangent = inputs
    inner = HEADS * HEAD
    flat_weight = kv_weight.reshape(D, 2 * inner)
    key_value = jnp.dot(states.reshape(ROWS * LEN_ENC, D), flat_weight, preferred_element_type=jnp.float32)
    key_value = lax.optimization_barrier(key_value.astype(jnp.bfloat16)).astype(jnp.float32)
    key_value = key_value.reshape(ROWS, LEN_ENC, 2, HEADS, HEAD)
    key_part = key_value[:, :, 0]
    value_part = key_value[:, :, 1]
    query_heads = queries.reshape(ROWS, LEN_DEC, HEADS, HEAD).astype(jnp.float32)
    scores = jnp.einsum("rqhd,rkhd->rhqk", query_heads, key_part)
    same_segment = (query_segments[:, :, None] == key_segments[:, None, :])[:, None]
    exponent = jnp.where(same_segment, jnp.exp(scores), 0.0)
    attention = exponent / jnp.sum(exponent, axis=-1, keepdims=True)
    rounded_attention = lax.optimization_barrier(attention.astype(jnp.bfloat16)).astype(jnp.float32)
    context = jnp.einsum("rhqk,rkhd->rqhd", rounded_attention, value_part).astype(jnp.bfloat16)
    context_grad = ctx_cotangent.reshape(ROWS, LEN_DEC, HEADS, HEAD).astype(jnp.float32)
    attention_grad = jnp.einsum("rqhd,rkhd->rhqk", context_grad, value_part)
    score_grad = attention * (attention_grad - jnp.sum(attention * attention_grad, axis=-1, keepdims=True))
    rounded_score = lax.optimization_barrier(score_grad.astype(jnp.bfloat16)).astype(jnp.float32)
    key_grad = jnp.einsum("rhqk,rqhd->rkhd", rounded_score, query_heads)
    value_grad = jnp.einsum("rhqk,rqhd->rkhd", rounded_attention, context_grad)
    key_value_grad = jnp.stack([key_grad, value_grad], axis=2).astype(jnp.bfloat16)
    groups = HEADS // H_DEV
    group_width = H_DEV * HEAD
    grad_rows = key_value_grad.reshape(ROWS * LEN_ENC, 2, groups, group_width)
    weight_groups = kv_weight.reshape(D, 2, groups, group_width)
    state_total = jnp.zeros((ROWS * LEN_ENC, D), jnp.float32)
    for group in range(groups):
        group_grad = grad_rows[:, :, group].reshape(ROWS * LEN_ENC, 2 * group_width)
        group_weight = weight_groups[:, :, group].reshape(D, 2 * group_width)
        partial_value = jnp.dot(group_grad, group_weight.T, preferred_element_type=jnp.float32)
        state_total = state_total + lax.optimization_barrier(partial_value.astype(jnp.bfloat16)).astype(jnp.float32)
    state_grad = state_total.astype(jnp.bfloat16).reshape(ROWS, LEN_ENC, D)
    flat_grad = key_value_grad.reshape(ROWS, LEN_ENC, 2 * inner)

    def add_row(running, pair):
        row_states, row_grad = pair
        term = jnp.dot(row_states.T, row_grad, preferred_element_type=jnp.float32)
        return running + lax.optimization_barrier(term.astype(jnp.bfloat16)).astype(jnp.float32), None

    total, unused = lax.scan(add_row, jnp.zeros((D, 2 * inner), jnp.float32), (states, flat_grad))
    weight_grad = (total / ROWS).astype(jnp.bfloat16).reshape(D, 2, inner)
    return context.reshape(ROWS, LEN_DEC, inner), state_grad, weight_grad


def reference(enc_states, queries, query_segments, key_segments, kv_weight, ctx_cotangent):
    halfway = SECTIONS // 2
    states = jnp.roll(enc_states, halfway, axis=0)
    context, state_grad, weight_grad = lax.map(section, (states, queries, query_segments, key_segments, kv_weight, ctx_cotangent))
    return context, jnp.roll(state_grad, halfway, axis=0), weight_grad
```

```python
import functools

import jax
import jax.numpy as jnp
from jax import lax
from jax.experimental import pallas as pl
from jax.experimental.pallas import tpu as pltpu
from jax.sharding import PartitionSpec as P

HEAD = 64
IN_COLS = 128
OUT_COLS = 256
AHEAD = 3
LAG = 2
MESH = pl.DeviceIdType.MESH
NT = (((1,), (1,)), ((), ()))
TN = (((0,), (0,)), ((), ()))


def dot(a, b, dims=(((1,), (0,)), ((), ()))):
    return lax.dot_general(a, b, dims, preferred_element_type=jnp.float32)


def kernel(
    phases,
    rings,
    parts,
    enc,
    queries,
    query_segments,
    key_segments,
    weight,
    cotangent,
    ctx_out,
    state_out,
    weight_out,
    held,
    raw,
    flat,
    acc,
    stacked_q,
    stacked_c,
    mask,
    att,
    grad,
    partial,
    mp_in,
    total,
    wpart,
    pair_in,
    keep,
    x_out,
    x_in,
    raw_sem,
    in_send,
    in_recv,
    fwd_send,
    fwd_recv,
    mp_send,
    mp_recv,
    out_send,
    out_recv,
    pair_send,
    pair_recv,
    x_send,
    x_recv,
):
    keys, model = enc.shape
    tokens, width = queries.shape
    heads = width // HEAD
    chips = rings // 2
    chunks = model // IN_COLS
    share = chunks // parts
    steps = model // OUT_COLS
    block = chunks // rings
    pairs = chunks // 2
    rows = keys // parts
    phase, ring, part = lax.axis_index("phase"), lax.axis_index("dp"), lax.axis_index("mp")
    chip, core = ring // 2, ring % 2
    across = {"phase": (phase + phases // 2) % phases}
    others = [(part + 1 + j) % parts for j in range(parts - 1)]
    buddy = {"dp": chip * 2 + 1 - core}
    far = [((chip + 1 + j) % chips) * 2 + core for j in range(chips - 1)]

    barrier = pltpu.get_barrier_semaphore()
    greeted = [across, buddy] + [{"mp": o} for o in others] + [{"dp": f} for f in far]
    for device in greeted:
        pl.semaphore_signal(barrier, inc=1, device_id=device, device_id_type=MESH)

    load = pltpu.make_async_copy(weight, raw, raw_sem)
    load.start()

    def remote(src, dst, send, recv, device):
        return pltpu.make_async_remote_copy(
            src_ref=src, dst_ref=dst, send_sem=send, recv_sem=recv,
            device_id=device, device_id_type=MESH,
        )

    def cols(i, size):
        return pl.ds(pl.multiple_of(i * size, size), size)

    def incoming(k):
        g = part * share + k
        return remote(
            enc.at[:, cols(g, IN_COLS)], held.at[g], in_send.at[k], in_recv.at[k], across
        )

    def forward(k, j):
        g = part * share + k
        return remote(
            held.at[g], held.at[g], fwd_send.at[j * share + k], fwd_recv.at[g], {"mp": others[j]}
        )

    def forwarded(k, j):
        g = others[j] * share + k
        return remote(
            held.at[g], held.at[g], fwd_send.at[j * share + k], fwd_recv.at[g], {"mp": others[j]}
        )

    def mp_out(n, j):
        return remote(
            partial.at[n, cols(others[j], rows), :], mp_in.at[part, n],
            mp_send.at[j * steps + n], mp_recv.at[part * steps + n], {"mp": others[j]},
        )

    def mp_arrived(n, j):
        return remote(
            mp_in.at[others[j], n], mp_in.at[others[j], n],
            mp_send.at[j * steps + n], mp_recv.at[others[j] * steps + n], {"mp": others[j]},
        )

    def outgoing(n):
        return remote(
            total.at[n], state_out.at[:, cols(n, OUT_COLS)], out_send.at[n], out_recv.at[n], across
        )

    def kept(t, parity):
        owner = (chip + 1 + t // block) % chips
        return (owner * 2 + parity) * block + t % block

    def pair(t):
        return remote(
            wpart.at[kept(t, 1 - core)], pair_in.at[t], pair_send.at[t], pair_recv.at[t], buddy
        )

    def crossing(t, device):
        return remote(x_out.at[t], x_in.at[t], x_send.at[t], x_recv.at[t], device)

    def far_of(t):
        return {"dp": ((chip + 1 + t // block) % chips) * 2 + core}

    pl.semaphore_wait(barrier, len(greeted))
    for k in range(min(AHEAD, share)):
        incoming(k).start()

    head_of = lax.broadcasted_iota(jnp.int32, (tokens, width), 1) // HEAD
    for ref, out in ((queries, stacked_q), (cotangent, stacked_c)):
        values = ref[...].astype(jnp.float32)
        for h in range(heads):
            out[h * tokens : (h + 1) * tokens] = jnp.where(head_of == h, values, 0.0).astype(
                jnp.bfloat16
            )
    of_key = jnp.broadcast_to(key_segments[...].astype(jnp.float32), (tokens, keys)).T
    of_query = jnp.broadcast_to(query_segments[...].astype(jnp.float32), (keys, tokens))
    mask[...] = jnp.where(of_key == of_query, 1.0, 0.0)
    acc[...] = jnp.zeros_like(acc)
    load.wait()

    def relay(g):
        here = cols(g, IN_COLS)
        both = raw[here]
        flat[here, :width] = both[:, 0, :]
        flat[here, width:] = both[:, 1, :]

    def project(g):
        acc[...] += dot(held[g], flat[cols(g, IN_COLS), :])

    def arrive(k, carry):
        relay(part * share + k)
        for o in others:
            relay(o * share + k)
        incoming(k).wait_recv()
        for j in range(parts - 1):
            forward(k, j).start()
        incoming(k).wait_send()

        @pl.when(k + AHEAD < share)
        def _():
            incoming(k + AHEAD).start()

        project(part * share + k)

        @pl.when(k > 0)
        def _():
            for j in range(parts - 1):
                forwarded(k - 1, j).wait_recv()
                project(others[j] * share + k - 1)

        return carry

    lax.fori_loop(0, share, arrive, 0)
    for j in range(parts - 1):
        forwarded(share - 1, j).wait_recv()
        project(others[j] * share + share - 1)

    key_part = acc[:, :width].astype(jnp.bfloat16)
    value_part = acc[:, width:].astype(jnp.bfloat16)
    shown = mask[...] > 0.5
    for h in range(heads):
        here = slice(h * tokens, (h + 1) * tokens)
        exponent = jnp.where(shown, jnp.exp(dot(key_part, stacked_q[here], NT)), 0.0)
        attention = exponent * (1.0 / jnp.sum(exponent, axis=0, keepdims=True))
        attention_grad = dot(value_part, stacked_c[here], NT)
        score_grad = attention * (
            attention_grad - jnp.sum(attention * attention_grad, axis=0, keepdims=True)
        )
        att[0, :, here] = score_grad.astype(jnp.bfloat16)
        att[1, :, here] = attention.astype(jnp.bfloat16)
    grad[:, :width] = dot(att[0], stacked_q[...]).astype(jnp.bfloat16)
    grad[:, width:] = dot(att[1], stacked_c[...]).astype(jnp.bfloat16)

    def weigh(g):
        wpart[g] = dot(held[g], grad[...], TN).astype(jnp.bfloat16)

    def back(n, carry):
        @pl.when(n < steps)
        def _():
            partial[n] = dot(grad[...], flat[cols(n, OUT_COLS), :], NT).astype(jnp.bfloat16)
            for j in range(parts - 1):
                mp_out(n, j).start()

        @pl.when(n < pairs)
        def _():
            weigh(kept(n, 1 - core))
            pair(n).start()

        @pl.when(jnp.logical_and(n >= LAG, n < steps + LAG))
        def _():
            old = n - LAG
            summed = partial[old, cols(part, rows), :].astype(jnp.float32)
            for j in range(parts - 1):
                mp_arrived(old, j).wait_recv()
                summed = summed + mp_in[others[j], old].astype(jnp.float32)
            total[old] = summed.astype(jnp.bfloat16)
            outgoing(old).start()

        @pl.when(n < pairs)
        def _():
            weigh(kept(n, core))

        @pl.when(jnp.logical_and(n >= LAG, n < pairs + LAG))
        def _():
            old = n - LAG
            pair(old).wait_recv()
            summed = wpart[kept(old, core)].astype(jnp.float32) + pair_in[old].astype(jnp.float32)

            @pl.when(old < pairs - block)
            def _():
                x_out[old] = summed.astype(jnp.bfloat16)
                crossing(old, far_of(old)).start()

            @pl.when(old >= pairs - block)
            def _():
                keep[old - (pairs - block)] = summed

        return carry

    lax.fori_loop(0, max(steps, pairs) + LAG, back, 0)

    context = jnp.zeros((tokens, width), jnp.float32)
    for h in range(heads):
        one = dot(att[1, :, h * tokens : (h + 1) * tokens], value_part, TN)
        context = jnp.where(head_of == h, one, context)
    ctx_out[...] = context.astype(jnp.bfloat16)

    def finish(q, carry):
        summed = keep[q]
        for j in range(chips - 1):
            crossing(j * block + q, {"dp": far[j]}).wait_recv()
            summed = summed + x_in[j * block + q].astype(jnp.float32)
        weight_out[cols(q, IN_COLS), :] = (summed * (1.0 / rings)).astype(jnp.bfloat16)
        return carry

    lax.fori_loop(0, block, finish, 0)

    def drain(count, one):
        def step(i, carry):
            one(i)
            return carry

        lax.fori_loop(0, count, step, 0)

    for j in range(parts - 1):
        drain(share, lambda k: forward(k, j).wait_send())
        drain(steps, lambda n: mp_out(n, j).wait_send())
    drain(pairs, lambda t: pair(t).wait_send())
    if chips > 1:
        drain(pairs - block, lambda t: crossing(t, far_of(t)).wait_send())
    drain(steps, lambda n: outgoing(n).wait())


def body(enc_states, queries, query_segments, key_segments, kv_weight, ctx_cotangent):
    phases, rings, parts = (lax.axis_size(a) for a in ("phase", "dp", "mp"))
    keys, model = enc_states.shape[2:]
    tokens, width = queries.shape[2:]
    heads = width // HEAD
    chunks = model // IN_COLS
    share, steps, block, pairs = (
        chunks // parts, model // OUT_COLS, chunks // rings, chunks // 2,
    )
    rows = keys // parts
    crossed = max(pairs - block, 1)
    b16, f32 = jnp.bfloat16, jnp.float32
    vmem = pl.BlockSpec(memory_space=pltpu.VMEM)
    hbm = pl.BlockSpec(memory_space=pl.ANY)
    dma = pltpu.SemaphoreType.DMA
    context, state_grad, weight_grad = pl.pallas_call(
        functools.partial(kernel, phases, rings, parts),
        out_shape=(
            jax.ShapeDtypeStruct((tokens, width), b16),
            jax.ShapeDtypeStruct((rows, model), b16),
            jax.ShapeDtypeStruct((model // rings, 2 * width), b16),
        ),
        in_specs=[hbm, vmem, vmem, vmem, hbm, vmem],
        out_specs=(vmem, hbm, vmem),
        scratch_shapes=[
            pltpu.VMEM((chunks, keys, IN_COLS), b16),
            pltpu.VMEM((model, 2, width), b16),
            pltpu.VMEM((model, 2 * width), b16),
            pltpu.VMEM((keys, 2 * width), f32),
            pltpu.VMEM((heads * tokens, width), b16),
            pltpu.VMEM((heads * tokens, width), b16),
            pltpu.VMEM((keys, tokens), f32),
            pltpu.VMEM((2, keys, heads * tokens), b16),
            pltpu.VMEM((keys, 2 * width), b16),
            pltpu.VMEM((steps, keys, OUT_COLS), b16),
            pltpu.VMEM((parts, steps, rows, OUT_COLS), b16),
            pltpu.VMEM((steps, rows, OUT_COLS), b16),
            pltpu.VMEM((chunks, IN_COLS, 2 * width), b16),
            pltpu.VMEM((pairs, IN_COLS, 2 * width), b16),
            pltpu.VMEM((block, IN_COLS, 2 * width), f32),
            pltpu.VMEM((crossed, IN_COLS, 2 * width), b16),
            pltpu.VMEM((crossed, IN_COLS, 2 * width), b16),
            dma,
            dma((share,)),
            dma((share,)),
            dma(((parts - 1) * share,)),
            dma((chunks,)),
            dma(((parts - 1) * steps,)),
            dma((parts * steps,)),
            dma((steps,)),
            dma((steps,)),
            dma((pairs,)),
            dma((pairs,)),
            dma((crossed,)),
            dma((crossed,)),
        ],
        compiler_params=pltpu.CompilerParams(
            collective_id=0, has_side_effects=True, vmem_limit_bytes=56 * 2**20
        ),
        cost_estimate=pl.CostEstimate(
            flops=12 * keys * model * width, bytes_accessed=9 * 2**20, transcendentals=0
        ),
    )(
        enc_states[0, 0], queries[0, 0], query_segments[0], key_segments[0],
        kv_weight[0], ctx_cotangent[0, 0],
    )
    return (
        context[None, None],
        state_grad[None, None],
        weight_grad.reshape(1, -1, 2, width),
    )


def solution(mesh):
    placed = (
        P("phase", "dp", None, None),
        P("phase", "dp", None, "mp"),
        P("phase", "dp", None),
        P("phase", "dp", None),
        P("phase", None, None, "mp"),
        P("phase", "dp", None, "mp"),
    )
    return jax.shard_map(
        body,
        mesh=mesh,
        in_specs=placed,
        out_specs=(
            P("phase", "dp", None, "mp"),
            P("phase", "dp", "mp", None),
            P("phase", "dp", None, "mp"),
        ),
        check_vma=False,
    )
```

```python
import functools

import jax
import jax.numpy as jnp
from jax import lax
from jax.experimental import pallas as pl
from jax.experimental.pallas import tpu as pltpu
from jax.sharding import PartitionSpec as P

HEAD = 64
IN_COLS = 128
OUT_COLS = 256
AHEAD = 3
EARLY = 9
LAG = 2
PAIR_LAG = 1
PIECES = 2
MESH = pl.DeviceIdType.MESH
NT = (((1,), (1,)), ((), ()))
TN = (((0,), (0,)), ((), ()))


def dot(a, b, dims=(((1,), (0,)), ((), ()))):
    return lax.dot_general(a, b, dims, preferred_element_type=jnp.float32)


def kernel(
    phases,
    rings,
    parts,
    enc,
    queries,
    query_segments,
    key_segments,
    weight,
    cotangent,
    ctx_out,
    state_out,
    weight_out,
    held,
    raw,
    flat,
    acc,
    stacked_q,
    stacked_c,
    mask,
    att,
    grad,
    partial,
    mp_in,
    total,
    wpart,
    pair_in,
    keep,
    x_out,
    x_in,
    raw_sem,
    in_send,
    in_recv,
    fwd_send,
    fwd_recv,
    mp_send,
    mp_recv,
    out_send,
    out_recv,
    pair_send,
    pair_recv,
    x_send,
    x_recv,
    final_ctx,
    final_weight,
    ctx_sem,
    weight_sem,
    turn,
):
    keys, model = enc.shape
    tokens, width = queries.shape
    heads = width // HEAD
    chips = rings // 2
    chunks = model // IN_COLS
    share = chunks // parts
    steps = model // OUT_COLS
    block = chunks // rings
    pairs = chunks // 2
    rows = keys // parts
    phase, ring, part = lax.axis_index("phase"), lax.axis_index("dp"), lax.axis_index("mp")
    chip, core = ring // 2, ring % 2
    across = {"phase": (phase + phases // 2) % phases}
    others = [(part + 1 + j) % parts for j in range(parts - 1)]
    buddy = {"dp": chip * 2 + 1 - core}
    far = [((chip + 1 + j) % chips) * 2 + core for j in range(chips - 1)]

    barrier = pltpu.get_barrier_semaphore()
    staggered = phases % 4 == 0
    odd = phase % 2 == 1
    beside = {"phase": phase + 1 - 2 * (phase % 2)}
    greeted = [across, buddy] + ([beside] if staggered else []) + [{"mp": o} for o in others] + [{"dp": f} for f in far]
    for device in greeted:
        pl.semaphore_signal(barrier, inc=1, device_id=device, device_id_type=MESH)

    load = pltpu.make_async_copy(weight, raw, raw_sem)
    load.start()

    def remote(src, dst, send, recv, device):
        return pltpu.make_async_remote_copy(
            src_ref=src, dst_ref=dst, send_sem=send, recv_sem=recv,
            device_id=device, device_id_type=MESH,
        )

    def cols(i, size):
        return pl.ds(pl.multiple_of(i * size, size), size)

    def incoming(k):
        g = part * share + k
        return remote(
            enc.at[:, cols(g, IN_COLS)], held.at[g], in_send.at[k], in_recv.at[k], across
        )

    def forward(k, j):
        g = part * share + k
        return remote(
            held.at[g], held.at[g], fwd_send.at[j * share + k], fwd_recv.at[g], {"mp": others[j]}
        )

    def forwarded(k, j):
        g = others[j] * share + k
        return remote(
            held.at[g], held.at[g], fwd_send.at[j * share + k], fwd_recv.at[g], {"mp": others[j]}
        )

    def mp_out(n, j):
        return remote(
            partial.at[n, cols(others[j], rows), :], mp_in.at[part, n],
            mp_send.at[j * steps + n], mp_recv.at[part * steps + n], {"mp": others[j]},
        )

    def mp_arrived(n, j):
        return remote(
            mp_in.at[others[j], n], mp_in.at[others[j], n],
            mp_send.at[j * steps + n], mp_recv.at[others[j] * steps + n], {"mp": others[j]},
        )

    def outgoing(n):
        return remote(
            total.at[n], state_out.at[:, cols(n, OUT_COLS)], out_send.at[n], out_recv.at[n], across
        )

    def kept(t, parity):
        owner = (chip + 1 + t // block) % chips
        return (owner * 2 + parity) * block + t % block

    def pair(t):
        return remote(
            wpart.at[kept(t, 1 - core)], pair_in.at[t], pair_send.at[t], pair_recv.at[t], buddy
        )

    def crossing(t, device):
        return remote(x_out.at[t], x_in.at[t], x_send.at[t], x_recv.at[t], device)

    def far_of(t):
        return {"dp": ((chip + 1 + t // block) % chips) * 2 + core}

    pl.semaphore_wait(barrier, len(greeted))

    def begin():
        for k in range(min(AHEAD, share)):
            incoming(k).start()

    if staggered:
        pl.when(jnp.logical_not(odd))(begin)
    else:
        begin()

    head_of = lax.broadcasted_iota(jnp.int32, (tokens, width), 1) // HEAD
    for ref, out in ((queries, stacked_q), (cotangent, stacked_c)):
        values = ref[...].astype(jnp.float32)
        for h in range(heads):
            out[h * tokens : (h + 1) * tokens] = jnp.where(head_of == h, values, 0.0).astype(
                jnp.bfloat16
            )
    of_key = jnp.broadcast_to(key_segments[...].astype(jnp.float32), (tokens, keys)).T
    of_query = jnp.broadcast_to(query_segments[...].astype(jnp.float32), (keys, tokens))
    mask[...] = jnp.where(of_key == of_query, 1.0, 0.0)
    acc[...] = jnp.zeros_like(acc)
    load.wait()

    def relay(g):
        here = cols(g, IN_COLS)
        both = raw[here]
        flat[here, :width] = both[:, 0, :]
        flat[here, width:] = both[:, 1, :]

    def project(g):
        acc[...] += dot(held[g], flat[cols(g, IN_COLS), :])

    def relay_all(g, carry):
        relay(g)
        return carry

    if staggered:

        @pl.when(odd)
        def _():
            lax.fori_loop(0, chunks, relay_all, 0)
            pl.semaphore_wait(turn, 1)
            begin()

    eager = odd if staggered else phase >= 0

    def arrive(k, carry):
        @pl.when(jnp.logical_not(odd) if staggered else eager)
        def _():
            relay(part * share + k)
            for o in others:
                relay(o * share + k)

        incoming(k).wait_recv()
        for j in range(parts - 1):
            forward(k, j).start()
        incoming(k).wait_send()

        @pl.when(k + AHEAD < share)
        def _():
            incoming(k + AHEAD).start()

        if staggered:

            @pl.when(jnp.logical_and(jnp.logical_not(odd), k == max(share - EARLY, 0)))
            def _():
                pl.semaphore_signal(turn, inc=1, device_id=beside, device_id_type=MESH)

        @pl.when(eager)
        def _():
            project(part * share + k)

        @pl.when(jnp.logical_and(k > 0, eager))
        def _():
            for j in range(parts - 1):
                forwarded(k - 1, j).wait_recv()
                project(others[j] * share + k - 1)

        return carry

    lax.fori_loop(0, share, arrive, 0)

    def catch_up(k, carry):
        @pl.when(jnp.logical_not(eager))
        def _():
            project(part * share + k)

        for j in range(parts - 1):
            forwarded(k, j).wait_recv()
            project(others[j] * share + k)
        return carry

    lax.fori_loop(jnp.where(eager, share - 1, 0), share, catch_up, 0)

    key_part = acc[:, :width].astype(jnp.bfloat16)
    value_part = acc[:, width:].astype(jnp.bfloat16)
    shown = mask[...] > 0.5
    for h in range(heads):
        here = slice(h * tokens, (h + 1) * tokens)
        exponent = jnp.where(shown, jnp.exp(dot(key_part, stacked_q[here], NT)), 0.0)
        attention = exponent * (1.0 / jnp.sum(exponent, axis=0, keepdims=True))
        attention_grad = dot(value_part, stacked_c[here], NT)
        score_grad = attention * (
            attention_grad - jnp.sum(attention * attention_grad, axis=0, keepdims=True)
        )
        att[0, :, here] = score_grad.astype(jnp.bfloat16)
        att[1, :, here] = attention.astype(jnp.bfloat16)
    grad[:, :width] = dot(att[0], stacked_q[...]).astype(jnp.bfloat16)
    grad[:, width:] = dot(att[1], stacked_c[...]).astype(jnp.bfloat16)

    def weigh(g):
        wpart[g] = dot(held[g], grad[...], TN).astype(jnp.bfloat16)

    def back(n, carry):
        @pl.when(n < steps)
        def _():
            partial[n] = dot(grad[...], flat[cols(n, OUT_COLS), :], NT).astype(jnp.bfloat16)
            for j in range(parts - 1):
                mp_out(n, j).start()

        @pl.when(jnp.logical_and(n >= LAG, n < steps + LAG))
        def _():
            old = n - LAG
            summed = partial[old, cols(part, rows), :].astype(jnp.float32)
            for j in range(parts - 1):
                mp_arrived(old, j).wait_recv()
                summed = summed + mp_in[others[j], old].astype(jnp.float32)
            total[old] = summed.astype(jnp.bfloat16)
            outgoing(old).start()

        at = n - LAG

        @pl.when(jnp.logical_and(at >= 0, at < pairs))
        def _():
            weigh(kept(at, 1 - core))
            pair(at).start()
            weigh(kept(at, core))

        @pl.when(jnp.logical_and(at >= PAIR_LAG, at < pairs + PAIR_LAG))
        def _():
            old = at - PAIR_LAG
            pair(old).wait_recv()
            summed = wpart[kept(old, core)].astype(jnp.float32) + pair_in[old].astype(jnp.float32)

            @pl.when(old < pairs - block)
            def _():
                x_out[old] = summed.astype(jnp.bfloat16)
                crossing(old, far_of(old)).start()

            @pl.when(old >= pairs - block)
            def _():
                keep[old - (pairs - block)] = summed

        return carry

    lax.fori_loop(0, max(steps, pairs + PAIR_LAG) + LAG, back, 0)

    context = jnp.zeros((tokens, width), jnp.float32)
    for h in range(heads):
        one = dot(att[1, :, h * tokens : (h + 1) * tokens], value_part, TN)
        context = jnp.where(head_of == h, one, context)
    final_ctx[...] = context.astype(jnp.bfloat16)
    ctx_copy = pltpu.make_async_copy(final_ctx, ctx_out, ctx_sem)
    ctx_copy.start()

    def weight_copy(q):
        here = cols(q, IN_COLS)
        return pltpu.make_async_copy(final_weight.at[here], weight_out.at[here], weight_sem.at[q])

    def finish(q, carry):
        summed = keep[q]
        for j in range(chips - 1):
            crossing(j * block + q, {"dp": far[j]}).wait_recv()
            summed = summed + x_in[j * block + q].astype(jnp.float32)
        mean = (summed * (1.0 / rings)).astype(jnp.bfloat16)
        final_weight[cols(q, IN_COLS)] = mean.reshape(IN_COLS, 2, width)
        weight_copy(q).start()
        return carry

    lax.fori_loop(0, block, finish, 0)

    def drain(count, one):
        def step(i, carry):
            one(i)
            return carry

        lax.fori_loop(0, count, step, 0)

    for j in range(parts - 1):
        drain(share, lambda k: forward(k, j).wait_send())
        drain(steps, lambda n: mp_out(n, j).wait_send())
    drain(pairs, lambda t: pair(t).wait_send())
    if chips > 1:
        drain(pairs - block, lambda t: crossing(t, far_of(t)).wait_send())
    ctx_copy.wait()
    drain(block, lambda q: weight_copy(q).wait())
    drain(steps, lambda n: outgoing(n).wait())


def hand_over(ctx, state, weight, ctx_out, state_out, weight_out, ctx_buf, state_buf, weight_buf, sems):
    moves = []
    for src, buf, dst in (
        (ctx, ctx_buf, ctx_out), (state, state_buf, state_out), (weight, weight_buf, weight_out),
    ):
        pieces = 1 if src is ctx else PIECES
        size = src.shape[0] // pieces
        for p in range(pieces):
            here, i = pl.ds(p * size, size), len(moves)
            moves.append(
                (
                    pltpu.make_async_copy(src.at[here], buf.at[here], sems.at[0, i]),
                    pltpu.make_async_copy(buf.at[here], dst.at[here], sems.at[1, i]),
                )
            )
    for load, _ in moves:
        load.start()
    for load, store in moves:
        load.wait()
        store.start()
    for _, store in moves:
        store.wait()


def body(enc_states, queries, query_segments, key_segments, kv_weight, ctx_cotangent):
    phases, rings, parts = (lax.axis_size(a) for a in ("phase", "dp", "mp"))
    keys, model = enc_states.shape[2:]
    tokens, width = queries.shape[2:]
    heads = width // HEAD
    chunks = model // IN_COLS
    share, steps, block, pairs = (
        chunks // parts, model // OUT_COLS, chunks // rings, chunks // 2,
    )
    rows = keys // parts
    crossed = max(pairs - block, 1)
    b16, f32 = jnp.bfloat16, jnp.float32
    vmem = pl.BlockSpec(memory_space=pltpu.VMEM)
    hbm = pl.BlockSpec(memory_space=pl.ANY)
    dma = pltpu.SemaphoreType.DMA
    results = pl.pallas_call(
        functools.partial(kernel, phases, rings, parts),
        out_shape=(
            jax.ShapeDtypeStruct((tokens, width), b16),
            jax.ShapeDtypeStruct((rows, model), b16),
            jax.ShapeDtypeStruct((model // rings, 2, width), b16),
        ),
        in_specs=[hbm, vmem, vmem, vmem, hbm, vmem],
        out_specs=(hbm, hbm, hbm),
        scratch_shapes=[
            pltpu.VMEM((chunks, keys, IN_COLS), b16),
            pltpu.VMEM((model, 2, width), b16),
            pltpu.VMEM((model, 2 * width), b16),
            pltpu.VMEM((keys, 2 * width), f32),
            pltpu.VMEM((heads * tokens, width), b16),
            pltpu.VMEM((heads * tokens, width), b16),
            pltpu.VMEM((keys, tokens), f32),
            pltpu.VMEM((2, keys, heads * tokens), b16),
            pltpu.VMEM((keys, 2 * width), b16),
            pltpu.VMEM((steps, keys, OUT_COLS), b16),
            pltpu.VMEM((parts, steps, rows, OUT_COLS), b16),
            pltpu.VMEM((steps, rows, OUT_COLS), b16),
            pltpu.VMEM((chunks, IN_COLS, 2 * width), b16),
            pltpu.VMEM((pairs, IN_COLS, 2 * width), b16),
            pltpu.VMEM((block, IN_COLS, 2 * width), f32),
            pltpu.VMEM((crossed, IN_COLS, 2 * width), b16),
            pltpu.VMEM((crossed, IN_COLS, 2 * width), b16),
            dma,
            dma((share,)),
            dma((share,)),
            dma(((parts - 1) * share,)),
            dma((chunks,)),
            dma(((parts - 1) * steps,)),
            dma((parts * steps,)),
            dma((steps,)),
            dma((steps,)),
            dma((pairs,)),
            dma((pairs,)),
            dma((crossed,)),
            dma((crossed,)),
            pltpu.VMEM((tokens, width), b16),
            pltpu.VMEM((model // rings, 2, width), b16),
            dma,
            dma((block,)),
            pltpu.SemaphoreType.REGULAR,
        ],
        compiler_params=pltpu.CompilerParams(
            collective_id=0, has_side_effects=True, vmem_limit_bytes=56 * 2**20
        ),
        cost_estimate=pl.CostEstimate(
            flops=12 * keys * model * width, bytes_accessed=9 * 2**20, transcendentals=0
        ),
    )(
        enc_states[0, 0], queries[0, 0], query_segments[0], key_segments[0],
        kv_weight[0], ctx_cotangent[0, 0],
    )
    context, state_grad, weight_grad = pl.pallas_call(
        hand_over,
        out_shape=tuple(jax.ShapeDtypeStruct(r.shape, r.dtype) for r in results),
        in_specs=[hbm] * 3,
        out_specs=(hbm,) * 3,
        scratch_shapes=[pltpu.VMEM(r.shape, r.dtype) for r in results] + [dma((2, 2 * PIECES + 1))],
    )(*results)
    return context[None, None], state_grad[None, None], weight_grad[None]


def solution(mesh):
    placed = (
        P("phase", "dp", None, None),
        P("phase", "dp", None, "mp"),
        P("phase", "dp", None),
        P("phase", "dp", None),
        P("phase", None, None, "mp"),
        P("phase", "dp", None, "mp"),
    )
    return jax.shard_map(
        body,
        mesh=mesh,
        in_specs=placed,
        out_specs=(
            P("phase", "dp", None, "mp"),
            P("phase", "dp", "mp", None),
            P("phase", "dp", None, "mp"),
        ),
        check_vma=False,
    )
```

```python
import functools

import jax
import jax.numpy as jnp
from jax import lax
from jax.experimental import pallas as pl
from jax.experimental.pallas import tpu as pltpu
from jax.sharding import PartitionSpec as P

HEAD = 64
IN_COLS = 128
OUT_COLS = 256
AHEAD = 3
EARLY = 11
LAG = 2
PAIR_LAG = 1
WAIT = 2
PIECES = 2
MESH = pl.DeviceIdType.MESH
NT = (((1,), (1,)), ((), ()))
TN = (((0,), (0,)), ((), ()))


def dot(a, b, dims=(((1,), (0,)), ((), ()))):
    return lax.dot_general(a, b, dims, preferred_element_type=jnp.float32)


def kernel(
    phases,
    rings,
    parts,
    enc,
    queries,
    query_segments,
    key_segments,
    weight,
    cotangent,
    ctx_out,
    state_out,
    weight_out,
    held,
    raw,
    flat,
    acc,
    stacked_q,
    stacked_c,
    mask,
    att,
    grad,
    partial,
    mp_in,
    total,
    wpart,
    pair_in,
    keep,
    x_out,
    x_in,
    raw_sem,
    in_send,
    in_recv,
    fwd_send,
    fwd_recv,
    mp_send,
    mp_recv,
    out_send,
    out_recv,
    pair_send,
    pair_recv,
    x_send,
    x_recv,
    final_ctx,
    final_weight,
    ctx_sem,
    weight_sem,
    turn,
):
    keys, model = enc.shape
    tokens, width = queries.shape
    heads = width // HEAD
    chips = rings // 2
    in_cols = min(IN_COLS, model // rings)
    chunks = model // in_cols
    share = chunks // parts
    steps = model // OUT_COLS
    block = chunks // rings
    pairs = chunks // 2
    rows = keys // parts
    phase, ring, part = lax.axis_index("phase"), lax.axis_index("dp"), lax.axis_index("mp")
    chip, core = ring // 2, ring % 2
    across = {"phase": (phase + phases // 2) % phases}
    others = [(part + 1 + j) % parts for j in range(parts - 1)]
    buddy = {"dp": chip * 2 + 1 - core}
    far = [((chip + 1 + j) % chips) * 2 + core for j in range(chips - 1)]

    barrier = pltpu.get_barrier_semaphore()
    staggered = phases % 4 == 0
    odd = phase % 2 == 1
    beside = {"phase": phase + 1 - 2 * (phase % 2)}
    greeted = [across, buddy] + ([beside] if staggered else []) + [{"mp": o} for o in others] + [{"dp": f} for f in far]
    for device in greeted:
        pl.semaphore_signal(barrier, inc=1, device_id=device, device_id_type=MESH)

    load = pltpu.make_async_copy(weight, raw, raw_sem)
    load.start()

    def remote(src, dst, send, recv, device):
        return pltpu.make_async_remote_copy(
            src_ref=src, dst_ref=dst, send_sem=send, recv_sem=recv,
            device_id=device, device_id_type=MESH,
        )

    def cols(i, size):
        return pl.ds(pl.multiple_of(i * size, size), size)

    def incoming(k):
        g = part * share + k
        return remote(
            enc.at[:, cols(g, in_cols)], held.at[g], in_send.at[k], in_recv.at[k], across
        )

    def forward(k, j):
        g = part * share + k
        return remote(
            held.at[g], held.at[g], fwd_send.at[j * share + k], fwd_recv.at[g], {"mp": others[j]}
        )

    def forwarded(k, j):
        g = others[j] * share + k
        return remote(
            held.at[g], held.at[g], fwd_send.at[j * share + k], fwd_recv.at[g], {"mp": others[j]}
        )

    def mp_out(n, j):
        return remote(
            partial.at[n, cols(others[j], rows), :], mp_in.at[part, n],
            mp_send.at[j * steps + n], mp_recv.at[part * steps + n], {"mp": others[j]},
        )

    def mp_arrived(n, j):
        return remote(
            mp_in.at[others[j], n], mp_in.at[others[j], n],
            mp_send.at[j * steps + n], mp_recv.at[others[j] * steps + n], {"mp": others[j]},
        )

    def outgoing(n):
        return remote(
            total.at[n], state_out.at[:, cols(n, OUT_COLS)], out_send.at[n], out_recv.at[n], across
        )

    def kept(t, parity):
        owner = (chip + 1 + t // block) % chips
        return (owner * 2 + parity) * block + t % block

    def pair(t):
        return remote(
            wpart.at[kept(t, 1 - core)], pair_in.at[t], pair_send.at[t], pair_recv.at[t], buddy
        )

    def crossing(t, device):
        return remote(x_out.at[t], x_in.at[t], x_send.at[t], x_recv.at[t], device)

    def far_of(t):
        return {"dp": ((chip + 1 + t // block) % chips) * 2 + core}

    pl.semaphore_wait(barrier, len(greeted))

    def begin():
        for k in range(min(AHEAD, share)):
            incoming(k).start()

    if staggered:
        pl.when(jnp.logical_not(odd))(begin)
    else:
        begin()

    head_of = lax.broadcasted_iota(jnp.int32, (tokens, width), 1) // HEAD
    for ref, out in ((queries, stacked_q), (cotangent, stacked_c)):
        values = ref[...].astype(jnp.float32)
        for h in range(heads):
            out[h * tokens : (h + 1) * tokens] = jnp.where(head_of == h, values, 0.0).astype(
                jnp.bfloat16
            )
    of_key = jnp.broadcast_to(key_segments[...].astype(jnp.float32), (tokens, keys)).T
    of_query = jnp.broadcast_to(query_segments[...].astype(jnp.float32), (keys, tokens))
    mask[...] = jnp.where(of_key == of_query, 1.0, 0.0)
    acc[...] = jnp.zeros_like(acc)
    load.wait()

    def relay(g):
        here = cols(g, in_cols)
        both = raw[here]
        flat[here, :width] = both[:, 0, :]
        flat[here, width:] = both[:, 1, :]

    def project(g):
        acc[...] += dot(held[g], flat[cols(g, in_cols), :])

    def relay_all(g, carry):
        relay(g)
        return carry

    if staggered:

        @pl.when(odd)
        def _():
            lax.fori_loop(0, chunks, relay_all, 0)
            pl.semaphore_wait(turn, 1)
            begin()

    eager = odd if staggered else phase >= 0

    def arrive(k, carry):
        @pl.when(jnp.logical_not(odd) if staggered else eager)
        def _():
            relay(part * share + k)
            for o in others:
                relay(o * share + k)

        incoming(k).wait_recv()
        for j in range(parts - 1):
            forward(k, j).start()
        incoming(k).wait_send()

        @pl.when(k + AHEAD < share)
        def _():
            incoming(k + AHEAD).start()

        if staggered:

            @pl.when(jnp.logical_and(jnp.logical_not(odd), k == max(share - EARLY, 0)))
            def _():
                pl.semaphore_signal(turn, inc=1, device_id=beside, device_id_type=MESH)

        @pl.when(eager)
        def _():
            project(part * share + k)

        @pl.when(jnp.logical_and(k > 0, eager))
        def _():
            for j in range(parts - 1):
                forwarded(k - 1, j).wait_recv()
                project(others[j] * share + k - 1)

        return carry

    lax.fori_loop(0, share, arrive, 0)

    def catch_up(k, carry):
        @pl.when(jnp.logical_not(eager))
        def _():
            project(part * share + k)

        for j in range(parts - 1):
            forwarded(k, j).wait_recv()
            project(others[j] * share + k)
        return carry

    lax.fori_loop(jnp.where(eager, share - 1, 0), share, catch_up, 0)

    key_part = acc[:, :width].astype(jnp.bfloat16)
    value_part = acc[:, width:].astype(jnp.bfloat16)
    shown = mask[...] > 0.5
    for h in range(heads):
        here = slice(h * tokens, (h + 1) * tokens)
        exponent = jnp.where(shown, jnp.exp(dot(key_part, stacked_q[here], NT)), 0.0)
        attention = exponent * (1.0 / jnp.sum(exponent, axis=0, keepdims=True))
        attention_grad = dot(value_part, stacked_c[here], NT)
        score_grad = attention * (
            attention_grad - jnp.sum(attention * attention_grad, axis=0, keepdims=True)
        )
        att[0, :, here] = score_grad.astype(jnp.bfloat16)
        att[1, :, here] = attention.astype(jnp.bfloat16)
    grad[:, :width] = dot(att[0], stacked_q[...]).astype(jnp.bfloat16)
    grad[:, width:] = dot(att[1], stacked_c[...]).astype(jnp.bfloat16)

    def weigh(g):
        wpart[g] = dot(held[g], grad[...], TN).astype(jnp.bfloat16)

    def back(n, carry):
        @pl.when(n < steps)
        def _():
            partial[n] = dot(grad[...], flat[cols(n, OUT_COLS), :], NT).astype(jnp.bfloat16)
            for j in range(parts - 1):
                mp_out(n, j).start()

        @pl.when(jnp.logical_and(n >= LAG, n < steps + LAG))
        def _():
            old = n - LAG
            summed = partial[old, cols(part, rows), :].astype(jnp.float32)
            for j in range(parts - 1):
                mp_arrived(old, j).wait_recv()
                summed = summed + mp_in[others[j], old].astype(jnp.float32)
            total[old] = summed.astype(jnp.bfloat16)
            outgoing(old).start()

        at = n - shift

        @pl.when(jnp.logical_and(at >= 0, at < pairs))
        def _():
            weigh(kept(at, 1 - core))
            pair(at).start()
            weigh(kept(at, core))

        @pl.when(jnp.logical_and(at >= PAIR_LAG, at < pairs + PAIR_LAG))
        def _():
            old = at - PAIR_LAG
            pair(old).wait_recv()
            summed = wpart[kept(old, core)].astype(jnp.float32) + pair_in[old].astype(jnp.float32)

            @pl.when(old < pairs - block)
            def _():
                x_out[old] = summed.astype(jnp.bfloat16)
                crossing(old, far_of(old)).start()

            @pl.when(old >= pairs - block)
            def _():
                keep[old - (pairs - block)] = summed

        return carry

    shift = jnp.where(odd, LAG, steps // WAIT) if staggered else LAG
    lax.fori_loop(0, jnp.maximum(steps + LAG, pairs + PAIR_LAG + shift), back, 0)

    context = jnp.zeros((tokens, width), jnp.float32)
    for h in range(heads):
        one = dot(att[1, :, h * tokens : (h + 1) * tokens], value_part, TN)
        context = jnp.where(head_of == h, one, context)
    final_ctx[...] = context.astype(jnp.bfloat16)
    ctx_copy = pltpu.make_async_copy(final_ctx, ctx_out, ctx_sem)
    ctx_copy.start()

    def weight_copy(q):
        here = cols(q, in_cols)
        return pltpu.make_async_copy(final_weight.at[here], weight_out.at[here], weight_sem.at[q])

    def finish(q, carry):
        summed = keep[q]
        for j in range(chips - 1):
            crossing(j * block + q, {"dp": far[j]}).wait_recv()
            summed = summed + x_in[j * block + q].astype(jnp.float32)
        mean = (summed * (1.0 / rings)).astype(jnp.bfloat16)
        final_weight[cols(q, in_cols)] = mean.reshape(in_cols, 2, width)
        weight_copy(q).start()
        return carry

    lax.fori_loop(0, block, finish, 0)

    def drain(count, one):
        def step(i, carry):
            one(i)
            return carry

        lax.fori_loop(0, count, step, 0)

    for j in range(parts - 1):
        drain(share, lambda k: forward(k, j).wait_send())
        drain(steps, lambda n: mp_out(n, j).wait_send())
    drain(pairs, lambda t: pair(t).wait_send())
    if chips > 1:
        drain(pairs - block, lambda t: crossing(t, far_of(t)).wait_send())
    ctx_copy.wait()
    drain(block, lambda q: weight_copy(q).wait())
    drain(steps, lambda n: outgoing(n).wait())


def hand_over(ctx, state, weight, ctx_out, state_out, weight_out, ctx_buf, state_buf, weight_buf, sems):
    moves = []
    for src, buf, dst in (
        (ctx, ctx_buf, ctx_out), (state, state_buf, state_out), (weight, weight_buf, weight_out),
    ):
        pieces = 1 if src is ctx else PIECES
        size = src.shape[0] // pieces
        for p in range(pieces):
            here, i = pl.ds(p * size, size), len(moves)
            moves.append(
                (
                    pltpu.make_async_copy(src.at[here], buf.at[here], sems.at[0, i]),
                    pltpu.make_async_copy(buf.at[here], dst.at[here], sems.at[1, i]),
                )
            )
    for load, _ in moves:
        load.start()
    for load, store in moves:
        load.wait()
        store.start()
    for _, store in moves:
        store.wait()


def body(enc_states, queries, query_segments, key_segments, kv_weight, ctx_cotangent):
    phases, rings, parts = (lax.axis_size(a) for a in ("phase", "dp", "mp"))
    keys, model = enc_states.shape[2:]
    tokens, width = queries.shape[2:]
    heads = width // HEAD
    in_cols = min(IN_COLS, model // rings)
    chunks = model // in_cols
    share, steps, block, pairs = (
        chunks // parts, model // OUT_COLS, chunks // rings, chunks // 2,
    )
    rows = keys // parts
    crossed = max(pairs - block, 1)
    b16, f32 = jnp.bfloat16, jnp.float32
    vmem = pl.BlockSpec(memory_space=pltpu.VMEM)
    hbm = pl.BlockSpec(memory_space=pl.ANY)
    dma = pltpu.SemaphoreType.DMA
    results = pl.pallas_call(
        functools.partial(kernel, phases, rings, parts),
        out_shape=(
            jax.ShapeDtypeStruct((tokens, width), b16),
            jax.ShapeDtypeStruct((rows, model), b16),
            jax.ShapeDtypeStruct((model // rings, 2, width), b16),
        ),
        in_specs=[hbm, vmem, vmem, vmem, hbm, vmem],
        out_specs=(hbm, hbm, hbm),
        scratch_shapes=[
            pltpu.VMEM((chunks, keys, in_cols), b16),
            pltpu.VMEM((model, 2, width), b16),
            pltpu.VMEM((model, 2 * width), b16),
            pltpu.VMEM((keys, 2 * width), f32),
            pltpu.VMEM((heads * tokens, width), b16),
            pltpu.VMEM((heads * tokens, width), b16),
            pltpu.VMEM((keys, tokens), f32),
            pltpu.VMEM((2, keys, heads * tokens), b16),
            pltpu.VMEM((keys, 2 * width), b16),
            pltpu.VMEM((steps, keys, OUT_COLS), b16),
            pltpu.VMEM((parts, steps, rows, OUT_COLS), b16),
            pltpu.VMEM((steps, rows, OUT_COLS), b16),
            pltpu.VMEM((chunks, in_cols, 2 * width), b16),
            pltpu.VMEM((pairs, in_cols, 2 * width), b16),
            pltpu.VMEM((block, in_cols, 2 * width), f32),
            pltpu.VMEM((crossed, in_cols, 2 * width), b16),
            pltpu.VMEM((crossed, in_cols, 2 * width), b16),
            dma,
            dma((share,)),
            dma((share,)),
            dma(((parts - 1) * share,)),
            dma((chunks,)),
            dma(((parts - 1) * steps,)),
            dma((parts * steps,)),
            dma((steps,)),
            dma((steps,)),
            dma((pairs,)),
            dma((pairs,)),
            dma((crossed,)),
            dma((crossed,)),
            pltpu.VMEM((tokens, width), b16),
            pltpu.VMEM((model // rings, 2, width), b16),
            dma,
            dma((block,)),
            pltpu.SemaphoreType.REGULAR,
        ],
        compiler_params=pltpu.CompilerParams(
            collective_id=0, has_side_effects=True, vmem_limit_bytes=56 * 2**20
        ),
        cost_estimate=pl.CostEstimate(
            flops=12 * keys * model * width, bytes_accessed=9 * 2**20, transcendentals=0
        ),
    )(
        enc_states[0, 0], queries[0, 0], query_segments[0], key_segments[0],
        kv_weight[0], ctx_cotangent[0, 0],
    )
    context, state_grad, weight_grad = pl.pallas_call(
        hand_over,
        out_shape=tuple(jax.ShapeDtypeStruct(r.shape, r.dtype) for r in results),
        in_specs=[hbm] * 3,
        out_specs=(hbm,) * 3,
        scratch_shapes=[pltpu.VMEM(r.shape, r.dtype) for r in results] + [dma((2, 2 * PIECES + 1))],
    )(*results)
    return context[None, None], state_grad[None, None], weight_grad[None]


def solution(mesh):
    placed = (
        P("phase", "dp", None, None),
        P("phase", "dp", None, "mp"),
        P("phase", "dp", None),
        P("phase", "dp", None),
        P("phase", None, None, "mp"),
        P("phase", "dp", None, "mp"),
    )
    return jax.shard_map(
        body,
        mesh=mesh,
        in_specs=placed,
        out_specs=(
            P("phase", "dp", None, "mp"),
            P("phase", "dp", "mp", None),
            P("phase", "dp", None, "mp"),
        ),
        check_vma=False,
    )
```
